256 devices in a mesh: loop: 16 (over y, x), dp: 16 (over z, core).
Axes of the slice: x: 4, y: 4, z: 8, core: 2. Of those that a mesh axis runs over, the one named last changes fastest.
Arguments:
- tokens: bfloat16 [3584, 8192], P('dp', 'loop'), may hold values from -8 to 8
- weight: bfloat16 [8192, 14336], P('loop', 'dp'), as said below
- rounding: float32 [8192, 14336], P('loop', 'dp'), may hold values from -6 to 6
- floor_codes: int32 [8192, 14336], P('loop', 'dp'), may hold values from -1 to 15
- scale_codes: int32 [14336], P('dp'), may hold values from 12 to 15
- zero_codes: int32 [14336], P('dp'), may hold values from 0 to 15
- block_mask: int32 [128, 224], P('loop', 'dp'), may hold values from 0 to 1, as said below
Outputs:
- refined: float32 [8192, 14336], P('loop', 'dp')
The draws below stay inside these ranges and needn't reach their ends.
Inputs may be any that keep to these rules, and one draw needn't show every extreme that they name: weight equals scales times (floor_codes - zero_point + a fraction in [0, 1)), then is rounded to bfloat16. `block_mask`: the share of surviving blocks differs between column blocks.
All inputs are finite; a program needn't handle non-finite values.
Results may differ from the reference program's by a relative error of at most 0.019.
Values may be sent and summed in bfloat16 or wider, within the bound.
A program may use at most 128 MiB of HBM per device.

```python
import jax
import jax.numpy as jnp
from jax import lax

D = 8192
FF = 14336
BLOCK = 64
ITERS = 2
TOKENS = 3584
N_LOOP = 16


def grid_codes(key):
    floor_codes = jax.random.randint(jax.random.fold_in(key, 11), (D, FF), -1, 16, dtype=jnp.int32)
    scale_codes = jax.random.randint(jax.random.fold_in(key, 12), (FF,), 12, 16, dtype=jnp.int32)
    zero_codes = jax.random.randint(jax.random.fold_in(key, 13), (FF,), 0, 16, dtype=jnp.int32)
    return (floor_codes, scale_codes, zero_codes)


def draw_floor_codes(key, part):
    return grid_codes(key)[0]


def draw_scale_codes(key, part):
    return grid_codes(key)[1]


def draw_zero_codes(key, part):
    return grid_codes(key)[2]


def draw_weight(key, part):
    floor_codes, scale_codes, zero_codes = grid_codes(key)
    scales = 0.02 * jnp.exp2(scale_codes.astype(jnp.float32) * 0.25)
    fraction = jax.random.uniform(jax.random.fold_in(key, 14), (D, FF), jnp.float32, 0.0, 1.0)
    values = scales[None, :] * (floor_codes.astype(jnp.float32) - zero_codes.astype(jnp.float32)[None, :] + fraction)
    return values.astype(jnp.bfloat16)


def draw_block_mask(key, part):
    density = jax.random.randint(jax.random.fold_in(key, 21), (FF // BLOCK,), 1, 8, dtype=jnp.int32)
    rolled = jax.random.randint(jax.random.fold_in(key, 22), (D // BLOCK, FF // BLOCK), 0, 8, dtype=jnp.int32)
    return (rolled < density[None, :]).astype(jnp.int32)


def block_scale(key, extent, split, least, high):
    def one(position, shards_of):
        heights = jax.random.uniform(jax.random.fold_in(jax.random.fold_in(key, 6), position), (shards_of,), jnp.float32, least / len(split), high / len(split))
        return jnp.repeat(jnp.exp(heights), extent[position] // shards_of).reshape((-1,) + (1,) * (len(extent) - position - 1))

    loudness = one(*split[0])
    for cut in split[1:]:
        loudness = loudness * one(*cut)
    return loudness


def centred(key, extent, deviation, limit, pieces=(), held_as=jnp.bfloat16):
    level = block_scale(key, extent, pieces, -0.22, 0.18) if pieces else 1.0
    entries = jax.random.normal(key, extent, jnp.float32) * deviation * level
    return jnp.minimum(jnp.maximum(entries, -limit), limit).astype(held_as)


def setup_inputs(seed: int = 0) -> dict:
    streams_of = jax.random.split(jax.random.key(seed), 8)
    tokens = centred(streams_of[0], (TOKENS, D), 2.0, 8.0, ((0, 16), (1, 16)))
    weight = draw_weight(jax.random.fold_in(streams_of[7], 71), 0)
    rounding = centred(streams_of[2], (D, FF), 1.0, 6.0, ((0, 16), (1, 16)), jnp.float32)
    floor_codes = draw_floor_codes(jax.random.fold_in(streams_of[7], 71), 0)
    scale_codes = draw_scale_codes(jax.random.fold_in(streams_of[7], 71), 0)
    zero_codes = draw_zero_codes(jax.random.fold_in(streams_of[7], 71), 0)
    block_mask = draw_block_mask(jax.random.fold_in(streams_of[7], 71), 0)
    return {"tokens": tokens, "weight": weight, "rounding": rounding, "floor_codes": floor_codes, "scale_codes": scale_codes, "zero_codes": zero_codes, "block_mask": block_mask}


step_rate = 20.0
reg_weight = 0.05
base_scale = 0.02


def expand(block_mask):
    row_blocks, col_blocks = block_mask.shape
    spread = jnp.broadcast_to(block_mask[:, None, :, None], (row_blocks, BLOCK, col_blocks, BLOCK))
    return spread.reshape(row_blocks * BLOCK, col_blocks * BLOCK).astype(jnp.float32)


def refine(tokens, weight, rounding, floor_codes, scales, zero_point, kept_mask):
    panel_width = weight.shape[1]
    floors = floor_codes.astype(jnp.float32)
    in_range = ((floor_codes >= 0) & (floor_codes <= 14)).astype(jnp.float32)
    target = weight.astype(jnp.float32)
    grouped = tokens.astype(jnp.float32).reshape(TOKENS, N_LOOP, D // N_LOOP)
    for iteration in range(ITERS):
        relaxed = jax.nn.sigmoid(rounding)
        levels = jnp.clip(floors + relaxed, 0.0, 15.0)
        w_delta = (kept_mask * (scales[None, :] * (levels - zero_point[None, :]) - target)).astype(jnp.bfloat16)
        delta_groups = w_delta.astype(jnp.float32).reshape(N_LOOP, D // N_LOOP, panel_width)
        partials = jnp.einsum("tkd,kdc->ktc", grouped, delta_groups, precision=lax.Precision.HIGHEST)
        rounded = lax.optimization_barrier(partials.astype(jnp.bfloat16))
        residual = jnp.sum(rounded.astype(jnp.float32), axis=0)
        scaled_err = ((2.0 / TOKENS) * residual).astype(jnp.bfloat16)
        gradient = jnp.dot(tokens.T, scaled_err, preferred_element_type=jnp.float32)
        centered = 2.0 * relaxed - 1.0
        descent = gradient * scales[None, :] * in_range - reg_weight * 8.0 * centered ** 3
        rounding = rounding - step_rate * kept_mask * descent * relaxed * (1.0 - relaxed)
    return rounding


def reference(tokens, weight, rounding, floor_codes, scale_codes, zero_codes, block_mask):
    panel_width = FF // 8
    scales_all = base_scale * jnp.exp2(scale_codes.astype(jnp.float32) * 0.25)
    zero_all = zero_codes.astype(jnp.float32)

    def one_panel(panel_index):
        first_col = (panel_index * panel_width).astype(jnp.int32)
        first_block = (panel_index * (panel_width // BLOCK)).astype(jnp.int32)
        weight_panel = lax.dynamic_slice_in_dim(weight, first_col, panel_width, 1)
        rounding_panel = lax.dynamic_slice_in_dim(rounding, first_col, panel_width, 1)
        floor_panel = lax.dynamic_slice_in_dim(floor_codes, first_col, panel_width, 1)
        scale_panel = lax.dynamic_slice_in_dim(scales_all, first_col, panel_width, 0)
        zero_panel = lax.dynamic_slice_in_dim(zero_all, first_col, panel_width, 0)
        mask_panel = lax.dynamic_slice_in_dim(block_mask, first_block, panel_width // BLOCK, 1)
        return refine(tokens, weight_panel, rounding_panel, floor_panel, scale_panel, zero_panel, expand(mask_panel))

    panels = lax.map(one_panel, jnp.arange(8, dtype=jnp.int32))
    return jnp.transpose(panels, (1, 0, 2)).reshape(D, FF)
```

```python
import jax
import jax.numpy as jnp
from jax import lax
from jax.sharding import Mesh
from jax.sharding import PartitionSpec as P

BLOCK = 64
ITERS = 2


step_rate = 20.0
reg_weight = 0.05
base_scale = 0.02


def expand(block_mask):
    row_blocks, col_blocks = block_mask.shape
    spread = jnp.broadcast_to(block_mask[:, None, :, None], (row_blocks, BLOCK, col_blocks, BLOCK))
    return spread.reshape(row_blocks * BLOCK, col_blocks * BLOCK).astype(jnp.float32)


def token_product(token_rows, scaled_err):
    return lax.dot_general(
        token_rows, scaled_err, (((0,), (0,)), ((), ())), preferred_element_type=jnp.float32
    )


def per_device(tokens, weight, rounding, floor_codes, scale_codes, zero_codes, block_mask):
    gathered = lax.all_gather(tokens, ("z", "core"), axis=0, tiled=True)
    gathered = lax.all_gather(gathered, "y", axis=1, tiled=True)
    token_count = gathered.shape[0]
    scales = base_scale * jnp.exp2(scale_codes.astype(jnp.float32) * 0.25)
    zero_point = zero_codes.astype(jnp.float32)
    kept_mask = expand(block_mask)
    floors = floor_codes.astype(jnp.float32)
    in_range = ((floor_codes >= 0) & (floor_codes <= 14)).astype(jnp.float32)
    target = weight.astype(jnp.float32)
    for iteration in range(ITERS):
        relaxed = jax.nn.sigmoid(rounding)
        levels = jnp.clip(floors + relaxed, 0.0, 15.0)
        w_delta = (kept_mask * (scales[None, :] * (levels - zero_point[None, :]) - target)).astype(
            jnp.bfloat16
        )
        w_tall = lax.all_to_all(w_delta, "y", split_axis=1, concat_axis=0, tiled=True)
        partial_sum = jnp.dot(gathered, w_tall, preferred_element_type=jnp.float32)
        residual = lax.psum(partial_sum.astype(jnp.bfloat16), "x").astype(jnp.float32)
        scaled_err = (2.0 / token_count * residual).astype(jnp.bfloat16)
        grad_tall = token_product(gathered, scaled_err).astype(jnp.bfloat16)
        gradient = lax.all_to_all(grad_tall, "y", split_axis=0, concat_axis=1, tiled=True)
        gradient = gradient.astype(jnp.float32)
        centered = 2.0 * relaxed - 1.0
        descent = gradient * scales[None, :] * in_range - reg_weight * 8.0 * centered**3
        rounding = rounding - step_rate * kept_mask * descent * relaxed * (1.0 - relaxed)
    return rounding


def solution(mesh):
    fine = Mesh(mesh.devices.reshape(4, 4, 8, 2), ("y", "x", "z", "core"))
    loop, dp = ("y", "x"), ("z", "core")
    placed = (
        P(dp, loop),
        P(loop, dp),
        P(loop, dp),
        P(loop, dp),
        P(dp),
        P(dp),
        P(loop, dp),
    )
    return jax.shard_map(
        per_device, mesh=fine, in_specs=placed, out_specs=P(loop, dp), check_vma=False
    )
```

```python
import functools

import jax
import jax.numpy as jnp
from jax import lax
from jax.experimental import pallas as pl
from jax.experimental.pallas import tpu as pltpu
from jax.sharding import Mesh
from jax.sharding import PartitionSpec as P

BLOCK = 64
ITERS = 2
step_rate = 20.0
reg_weight = 0.05
base_scale = 0.02

NY, NX, NZ = 4, 4, 8
SIZES = {"y": NY, "x": NX, "z": NZ, "core": 2}
TOK = 3584
SH = 224
HALF = 112
CH = 448
FEAT = 512
COLS = 896
TILE = 224
UNIT = 32
F32, BF16 = jnp.float32, jnp.bfloat16


def neighbour(axis, offset):
    size = SIZES[axis]
    return {axis: lax.rem(lax.axis_index(axis) + offset + size, size)}


def remote(src, dst, send_sem, recv_sem, axis, offset):
    return pltpu.make_async_remote_copy(
        src_ref=src,
        dst_ref=dst,
        send_sem=send_sem,
        recv_sem=recv_sem,
        device_id=neighbour(axis, offset),
        device_id_type=pl.DeviceIdType.MESH,
    )


def kernel(
    tok_ref, w_ref, v_ref, fc_ref, sc_ref, zp_ref, kept_ref, out_ref,
    x_buf, vt, ft, tt, sct, zpt, w_out, w_all, r_out, r_in, s_all, g_acc, g_out, g_all,
    ya_s, ya_r, za_s, za_r, zb_s, zb_r, yb_s, yb_r, da_s, da_r, db_s, db_r,
    ws_s, ws_r, rs_s, rs_r, ag_s, ag_r, gs_s, gs_r,
):
    y, x, z, core = (lax.axis_index(name) for name in ("y", "x", "z", "core"))

    barrier = pltpu.get_barrier_semaphore()
    partners = [("y", d) for d in (1, 2, 3)] + [("x", d) for d in (1, 2, 3)]
    partners += [("z", 1), ("z", -1), ("core", 1)]
    for axis, offset in partners:
        pl.semaphore_signal(
            barrier, 1, device_id=neighbour(axis, offset), device_id_type=pl.DeviceIdType.MESH
        )
    pl.semaphore_wait(barrier, len(partners))

    def place(j):
        off = ((j + 1) // 2) * (1 - 2 * lax.rem(j, 2))
        return lax.rem(z + off + NZ, NZ)

    def part(zz, cc, b, first=0, rows=HALF):
        return pl.ds(pl.multiple_of((zz * 2 + cc) * SH + b * HALF + first, 16), rows)

    def y_a(d):
        ref = x_buf.at[y, part(z, core, 0)]
        return remote(ref, ref, ya_s.at[d - 1], ya_r.at[d - 1], "y", d)

    def z_a(j, direction):
        ref = x_buf.at[:, part(place_sent(j, direction), core, 0)]
        return remote(ref, ref, za_s.at[j], za_r.at[j], "z", direction)

    def z_a_last(h, direction):
        ref = x_buf.at[pl.ds(2 * h, 2), part(place_sent(NZ - 1, direction), core, 0)]
        return remote(ref, ref, za_s.at[NZ - 1 + h], za_r.at[NZ - 1 + h], "z", direction)

    def z_b(j, direction):
        ref = x_buf.at[y, part(place_sent(j, direction), core, 1)]
        return remote(ref, ref, zb_s.at[j], zb_r.at[j], "z", direction)

    def z_b_last(h, direction):
        ref = x_buf.at[y, part(place_sent(NZ - 1, direction), core, 1, 64 * h, (64, 48)[h])]
        return remote(ref, ref, zb_s.at[NZ - 1 + h], zb_r.at[NZ - 1 + h], "z", direction)

    def place_sent(j, direction):
        return lax.rem(z - direction * ((j + 1) // 2 - 1) + NZ, NZ)

    def y_b(j, d):
        ref = x_buf.at[y, part(place(j), core, 1)]
        return remote(ref, ref, yb_s.at[j, d - 1], yb_r.at[j, d - 1], "y", d)

    def sib(j, b, sems):
        ref = x_buf.at[:, part(place(j), core, b)]
        return remote(ref, ref, sems[0].at[j], sems[1].at[j], "core", 1)

    def rs(j, d):
        q = lax.rem(x + d, NX)
        src = r_out.at[j, pl.ds(pl.multiple_of(q * HALF, 16), HALF)]
        return remote(src, r_in.at[j, d - 1], rs_s.at[j, d - 1], rs_r.at[j, d - 1], "x", d)

    def ag(j, d):
        ref = s_all.at[j, pl.ds(pl.multiple_of(x * HALF, 16), HALF)]
        return remote(ref, ref, ag_s.at[j, d - 1], ag_r.at[j, d - 1], "x", d)

    def w_copy(it, d):
        b = lax.rem(y + d, NY)
        return remote(w_out.at[b], w_all.at[y], ws_s.at[it, d - 1], ws_r.at[it, d - 1], "y", d)

    def g_copy(it, d):
        b = lax.rem(y + d, NY)
        return remote(g_out.at[b], g_all.at[y], gs_s.at[it, d - 1], gs_r.at[it, d - 1], "y", d)

    x_buf[y, pl.ds(pl.multiple_of((z * 2 + core) * SH, SH), SH), :] = tok_ref[...]
    for d in (2, 1, 3):
        y_a(d).start()
    z_b(1, 1).start()
    z_b(2, -1).start()
    for d in (2, 1, 3):
        y_b(0, d).start()

    def turn(ct, carry):
        c0 = pl.multiple_of(ct * 128, 128)
        cols = pl.ds(c0, 128)
        scale = base_scale * jnp.exp2(sc_ref[:, cols].astype(F32) * 0.25)
        sct[cols, :] = jnp.broadcast_to(scale, (128, 128)).T
        zpt[cols, :] = jnp.broadcast_to(zp_ref[:, cols].astype(F32), (128, 128)).T
        for rt in range(FEAT // 128):
            rows = slice(rt * 128, rt * 128 + 128)
            vt[cols, rows] = v_ref[rows, cols].T
            ft[cols, rows] = fc_ref[rows, cols].astype(F32).T
            tt[cols, rows] = w_ref[rows, cols].astype(F32).T.astype(BF16)
        return carry

    lax.fori_loop(0, COLS // 128, turn, 0)

    def gather_step(j):
        @pl.when(j == 0)
        def _():
            for d in (1, 2, 3):
                y_a(d).wait_recv()
            z_a(1, 1).start()
            z_a(2, -1).start()

        direction = 2 * lax.rem(j, 2) - 1

        @pl.when((j > 0) & (j < NZ - 1))
        def _():
            z_b(j, direction).wait_recv()

        @pl.when((j > 0) & (j < NZ - 3))
        def _():
            z_b(j + 2, direction).start()

        @pl.when(j == NZ - 3)
        def _():
            z_b_last(0, 1).start()

        @pl.when(j == NZ - 2)
        def _():
            z_b_last(1, -1).start()

        @pl.when(j == NZ - 1)
        def _():
            z_b_last(0, 1).wait_recv()
            z_b_last(1, -1).wait_recv()

        @pl.when(j > 0)
        def _():
            for d in (2, 1, 3):
                y_b(j, d).start()

        @pl.when((j > 0) & (j < NZ - 1))
        def _():
            z_a(j, direction).wait_recv()

        @pl.when((j > 0) & (j < NZ - 3))
        def _():
            z_a(j + 2, direction).start()

        @pl.when(j == NZ - 3)
        def _():
            z_a_last(0, 1).start()

        @pl.when(j == NZ - 2)
        def _():
            z_a_last(1, -1).start()

        @pl.when(j == NZ - 1)
        def _():
            z_a_last(0, 1).wait_recv()
            z_a_last(1, -1).wait_recv()

        sib(j, 0, (da_s, da_r)).start()

    def sibling_step(j):
        for d in (1, 2, 3):
            y_b(j, d).wait_recv()
        sib(j, 1, (db_s, db_r)).start()

    def partial_step(j):
        rows = pl.ds(pl.multiple_of(place(j) * CH, CH), CH)
        acc = None
        for g in range(NY):
            term = lax.dot_general(
                x_buf[g, rows, :], w_all[g], (((1,), (1,)), ((), ())), preferred_element_type=F32
            )
            acc = term if acc is None else acc + term
        r_out[j] = acc.astype(BF16)
        for d in (2, 1, 3):
            rs(j, d).start()

    def sum_step(j):
        mine = pl.ds(pl.multiple_of(x * HALF, 16), HALF)
        total = r_out[j, mine, :].astype(F32)
        for d in (1, 2, 3):
            rs(j, d).wait_recv()
            total = total + r_in[j, d - 1].astype(F32)
        s_all[j, mine, :] = ((2.0 / TOK) * total).astype(BF16)
        for d in (2, 1, 3):
            ag(j, d).start()

    def gradient_step(j):
        for d in (1, 2, 3):
            ag(j, d).wait_recv()
            rs(j, d).wait_send()
            ag(j, d).wait_send()

        @pl.when(j == 0)
        def _():
            g_acc[...] = jnp.zeros_like(g_acc)

        rows = pl.ds(pl.multiple_of(place(j) * CH, CH), CH)
        turned = s_all[j].astype(F32).T.astype(BF16)
        for g in range(NY):
            g_acc[g] += jnp.dot(turned, x_buf[g, rows, :], preferred_element_type=F32)

    def columns(u, b):
        r0 = pl.multiple_of(b * TILE + u * UNIT, UNIT)
        rows = pl.ds(r0, UNIT)
        kept = jnp.concatenate([kept_ref[r0 // BLOCK]] * (UNIT // 8), axis=0)
        wide = lambda ref: jnp.concatenate([ref[rows, :]] * (FEAT // 128), axis=1)
        return rows, kept, wide(sct), wide(zpt)

    def delta(v, f, t, kept, scale, zero):
        levels = jnp.clip(f + jax.nn.sigmoid(v), 0.0, 15.0)
        return (kept * (scale * (levels - zero) - t)).astype(BF16)

    def first_delta(b, dst):
        def unit(u, carry):
            rows, kept, scale, zero = columns(u, b)
            here = pl.ds(pl.multiple_of(u * UNIT, UNIT), UNIT)
            dst[here, :] = delta(
                vt[rows, :], ft[rows, :], tt[rows, :].astype(F32), kept, scale, zero
            )
            return carry

        lax.fori_loop(0, TILE // UNIT, unit, 0)

    def update(b, dst):
        def unit(u, carry):
            rows, kept, scale, zero = columns(u, b)
            here = pl.ds(pl.multiple_of(u * UNIT, UNIT), UNIT)
            v, f = vt[rows, :], ft[rows, :]
            relaxed = jax.nn.sigmoid(v)
            in_range = ((f >= 0.0) & (f <= 14.0)).astype(F32)
            centered = 2.0 * relaxed - 1.0
            gradient = g_all[b, here, :].astype(F32)
            descent = gradient * scale * in_range - reg_weight * 8.0 * (
                centered * centered * centered
            )
            v = v - step_rate * kept * descent * relaxed * (1.0 - relaxed)
            vt[rows, :] = v
            if dst is not None:
                dst[here, :] = delta(v, f, tt[rows, :].astype(F32), kept, scale, zero)
            return carry

        lax.fori_loop(0, TILE // UNIT, unit, 0)

    def send_gradient(it):
        for d in (2, 1, 3):
            b = lax.rem(y + d, NY)
            g_out[b] = g_acc[b].astype(BF16)
            g_copy(it, d).start()
        g_all[y] = g_acc[y].astype(BF16)

    gather_step(0)
    for d in (2, 1, 3):
        b = lax.rem(y + d, NY)
        first_delta(b, w_out.at[b])
        w_copy(0, d).start()
    first_delta(y, w_all.at[y])

    def stage(s, carry):
        pl.when(s < NZ)(lambda: gather_step(s))
        pl.when((s >= 1) & (s < NZ + 1))(lambda: sibling_step(s - 1))

        @pl.when(s == 2)
        def _():
            for d in (1, 2, 3):
                w_copy(0, d).wait_recv()

        @pl.when((s >= 2) & (s < NZ + 2))
        def _():
            sib(s - 2, 0, (da_s, da_r)).wait_recv()
            sib(s - 2, 1, (db_s, db_r)).wait_recv()
            partial_step(s - 2)

        pl.when((s >= 3) & (s < NZ + 3))(lambda: sum_step(s - 3))
        pl.when(s >= 4)(lambda: gradient_step(s - 4))
        return carry

    lax.fori_loop(1, NZ + 4, stage, 0)
    send_gradient(0)
    for d in (1, 2, 3):
        w_copy(0, d).wait_send()
    update(y, w_all.at[y])
    for d in (1, 3, 2):
        g_copy(0, d).wait_recv()
        b = lax.rem(y - d + NY, NY)
        update(b, w_out.at[b])
        w_copy(1, NY - d).start()

    for d in (1, 2, 3):
        w_copy(1, d).wait_recv()

    def stage_two(s, carry):
        pl.when(s < NZ)(lambda: partial_step(s))
        pl.when((s >= 1) & (s < NZ + 1))(lambda: sum_step(s - 1))
        pl.when(s >= 3)(lambda: gradient_step(s - 3))
        return carry

    lax.fori_loop(0, NZ + 3, stage_two, 0)
    for d in (1, 2, 3):
        g_copy(0, d).wait_send()
    send_gradient(1)
    update(y, None)
    for d in (1, 3, 2):
        g_copy(1, d).wait_recv()
        update(lax.rem(y - d + NY, NY), None)

    def turn_back(ct, carry):
        cols = pl.ds(pl.multiple_of(ct * 128, 128), 128)
        for rt in range(FEAT // 128):
            rows = slice(rt * 128, rt * 128 + 128)
            out_ref[rows, cols] = vt[cols, rows].T
        return carry

    lax.fori_loop(0, COLS // 128, turn_back, 0)

    for d in (1, 2, 3):
        y_a(d).wait_send()
        w_copy(1, d).wait_send()
        g_copy(1, d).wait_send()
    for j in range(1, NZ - 1):
        z_a(j, 2 * (j % 2) - 1).wait_send()
        z_b(j, 2 * (j % 2) - 1).wait_send()
    for h in range(2):
        z_a_last(h, 1 - 2 * h).wait_send()
        z_b_last(h, 1 - 2 * h).wait_send()

    def drain(j, carry):
        for d in (1, 2, 3):
            y_b(j, d).wait_send()
        sib(j, 0, (da_s, da_r)).wait_send()
        sib(j, 1, (db_s, db_r)).wait_send()
        return carry

    lax.fori_loop(0, NZ, drain, 0)


def per_device(tokens, weight, rounding, floor_codes, scale_codes, zero_codes, block_mask):
    kept = jnp.broadcast_to(
        block_mask.T.astype(F32)[:, None, :, None], (COLS // BLOCK, 8, FEAT // BLOCK, BLOCK)
    ).reshape(COLS // BLOCK, 8, FEAT)
    dma = lambda *shape: pltpu.SemaphoreType.DMA(shape)
    pair = lambda *shape: [dma(*shape), dma(*shape)]
    vmem = pl.BlockSpec(memory_space=pltpu.VMEM)
    return pl.pallas_call(
        kernel,
        out_shape=jax.ShapeDtypeStruct((FEAT, COLS), F32),
        in_specs=[vmem] * 7,
        out_specs=vmem,
        scratch_shapes=[
            pltpu.VMEM((NY, TOK, FEAT), BF16),
            pltpu.VMEM((COLS, FEAT), F32),
            pltpu.VMEM((COLS, FEAT), F32),
            pltpu.VMEM((COLS, FEAT), BF16),
            pltpu.VMEM((COLS, 128), F32),
            pltpu.VMEM((COLS, 128), F32),
            pltpu.VMEM((NY, TILE, FEAT), BF16),
            pltpu.VMEM((NY, TILE, FEAT), BF16),
            pltpu.VMEM((NZ, CH, TILE), BF16),
            pltpu.VMEM((NZ, NX - 1, HALF, TILE), BF16),
            pltpu.VMEM((NZ, CH, TILE), BF16),
            pltpu.VMEM((NY, TILE, FEAT), F32),
            pltpu.VMEM((NY, TILE, FEAT), BF16),
            pltpu.VMEM((NY, TILE, FEAT), BF16),
            *pair(3), *pair(NZ + 1), *pair(NZ + 1), *pair(NZ, 3), *pair(NZ), *pair(NZ),
            *pair(ITERS, 3), *pair(NZ, 3), *pair(NZ, 3), *pair(ITERS, 3),
        ],
        compiler_params=pltpu.CompilerParams(
            collective_id=0, has_side_effects=True, vmem_limit_bytes=60 << 20
        ),
        cost_estimate=pl.CostEstimate(
            flops=4 * 2 * TOK * FEAT * COLS, bytes_accessed=8 << 20, transcendentals=4 * FEAT * COLS
        ),
        name="adaround",
    )(
        tokens, weight, rounding, floor_codes,
        scale_codes.reshape(1, COLS), zero_codes.reshape(1, COLS), kept,
    )


def solution(mesh):
    fine = Mesh(mesh.devices.reshape(NY, NX, NZ, 2), ("y", "x", "z", "core"))
    loop, dp = ("y", "x"), ("z", "core")
    placed = (
        P(dp, loop),
        P(loop, dp),
        P(loop, dp),
        P(loop, dp),
        P(dp),
        P(dp),
        P(loop, dp),
    )
    return jax.shard_map(
        per_device, mesh=fine, in_specs=placed, out_specs=P(loop, dp), check_vma=False
    )
```

```python
import functools

import jax
import jax.numpy as jnp
from jax import lax
from jax.experimental import pallas as pl
from jax.experimental.pallas import tpu as pltpu
from jax.sharding import Mesh
from jax.sharding import PartitionSpec as P

BLOCK = 64
ITERS = 2
step_rate = 20.0
reg_weight = 0.05
base_scale = 0.02

NY, NX, NZ = 4, 4, 8
SIZES = {"y": NY, "x": NX, "z": NZ, "core": 2}
TOK = 3584
SH = 224
HALF = 112
CH = 448
FEAT = 512
COLS = 896
TILE = 224
HC = 112
UNIT = 16
F32, BF16 = jnp.float32, jnp.bfloat16


def neighbour(axis, offset):
    size = SIZES[axis]
    return {axis: lax.rem(lax.axis_index(axis) + offset + size, size)}


def remote(src, dst, send_sem, recv_sem, axis, offset):
    return pltpu.make_async_remote_copy(
        src_ref=src,
        dst_ref=dst,
        send_sem=send_sem,
        recv_sem=recv_sem,
        device_id=neighbour(axis, offset),
        device_id_type=pl.DeviceIdType.MESH,
    )


def kernel(
    tok_ref, w_hbm, v_hbm, fc_hbm, sc_ref, zp_ref, mask_ref, out_ref,
    w_ref, v_ref, fc_ref,
    x_buf, vt, ft, tt, sct, zpt, kept_ref, w_out, w_all, r_out, r_in, s_all, g_acc, g_out, g_all,
    r2_out, r2_in, s2_all, in_sem,
    ya_s, ya_r, za_s, za_r, zb_s, zb_r, yb_s, yb_r, da_s, da_r, db_s, db_r,
    ws_s, ws_r, w2_s, w2_r, rs_s, rs_r, ag_s, ag_r, rs2_s, rs2_r, ag2_s, ag2_r, gs_s, gs_r,
):
    y, x, z, core = (lax.axis_index(name) for name in ("y", "x", "z", "core"))

    inputs = [
        pltpu.make_async_copy(src, dst, in_sem.at[i])
        for i, (src, dst) in enumerate(((v_hbm, v_ref), (fc_hbm, fc_ref), (w_hbm, w_ref)))
    ]
    for copy in inputs:
        copy.start()

    barrier = pltpu.get_barrier_semaphore()
    partners = [("y", d) for d in (1, 2, 3)] + [("x", d) for d in (1, 2, 3)]
    partners += [("z", 1), ("z", -1), ("core", 1)]
    for axis, offset in partners:
        pl.semaphore_signal(
            barrier, 1, device_id=neighbour(axis, offset), device_id_type=pl.DeviceIdType.MESH
        )
    pl.semaphore_wait(barrier, len(partners))

    def place(j):
        off = ((j + 1) // 2) * (1 - 2 * lax.rem(j, 2))
        return lax.rem(z + off + NZ, NZ)

    def part(zz, cc, b, first=0, rows=HALF):
        return pl.ds(pl.multiple_of((zz * 2 + cc) * SH + b * HALF + first, 16), rows)

    def y_a(d):
        ref = x_buf.at[y, part(z, core, 0)]
        return remote(ref, ref, ya_s.at[d - 1], ya_r.at[d - 1], "y", d)

    def z_a(j, d, direction):
        ref = x_buf.at[lax.rem(y - d + NY, NY), part(place_sent(j, direction), core, 0)]
        return remote(ref, ref, za_s.at[j, d], za_r.at[j, d], "z", direction)

    def z_b(j, direction):
        ref = x_buf.at[y, part(place_sent(j, direction), core, 1)]
        return remote(ref, ref, zb_s.at[j], zb_r.at[j], "z", direction)

    def z_b_last(h, direction):
        ref = x_buf.at[y, part(place_sent(NZ - 1, direction), core, 1, 64 * h, (64, 48)[h])]
        return remote(ref, ref, zb_s.at[NZ - 1 + h], zb_r.at[NZ - 1 + h], "z", direction)

    def place_sent(j, direction):
        return lax.rem(z - direction * ((j + 1) // 2 - 1) + NZ, NZ)

    def y_b(j, d):
        ref = x_buf.at[y, part(place(j), core, 1)]
        return remote(ref, ref, yb_s.at[j, d - 1], yb_r.at[j, d - 1], "y", d)

    def sib(j, b, sems):
        ref = x_buf.at[:, part(place(j), core, b)]
        return remote(ref, ref, sems[0].at[j], sems[1].at[j], "core", 1)

    def rs(j, d):
        q = lax.rem(x + d, NX)
        src = r_out.at[j, pl.ds(pl.multiple_of(q * HALF, 16), HALF)]
        return remote(src, r_in.at[j, d - 1], rs_s.at[j, d - 1], rs_r.at[j, d - 1], "x", d)

    def ag(j, d):
        ref = s_all.at[j, pl.ds(pl.multiple_of(x * HALF, 16), HALF)]
        return remote(ref, ref, ag_s.at[j, d - 1], ag_r.at[j, d - 1], "x", d)

    def half(h, first=0):
        return pl.ds(pl.multiple_of(first + h * HC, 16), HC)

    def w_copy(d):
        b = lax.rem(y + d, NY)
        return remote(w_out.at[b], w_all.at[y], ws_s.at[d - 1], ws_r.at[d - 1], "y", d)

    def w2_copy(h, d):
        b = lax.rem(y + d, NY)
        src, dst = w_out.at[b, half(h)], w_all.at[y, half(h)]
        return remote(src, dst, w2_s.at[h, d - 1], w2_r.at[h, d - 1], "y", d)

    def g_copy(it, h, d):
        b = lax.rem(y + d, NY)
        src, dst = g_out.at[b, half(h)], g_all.at[y, half(h)]
        return remote(src, dst, gs_s.at[it, h, d - 1], gs_r.at[it, h, d - 1], "y", d)

    def rs2(u, d):
        q = lax.rem(x + d, NX)
        src = r2_out.at[u, pl.ds(pl.multiple_of(q * HALF, 16), HALF)]
        return remote(src, r2_in.at[u, d - 1], rs2_s.at[u, d - 1], rs2_r.at[u, d - 1], "x", d)

    def ag2(u, d):
        ref = s2_all.at[u, pl.ds(pl.multiple_of(x * HALF, 16), HALF)]
        return remote(ref, ref, ag2_s.at[u, d - 1], ag2_r.at[u, d - 1], "x", d)

    x_buf[y, pl.ds(pl.multiple_of((z * 2 + core) * SH, SH), SH), :] = tok_ref[...]
    for d in (2, 1, 3):
        y_a(d).start()
    z_b(1, 1).start()
    z_b(2, -1).start()
    z_a(1, 0, 1).start()
    z_a(2, 0, -1).start()
    for d in (2, 1, 3):
        y_b(0, d).start()

    def turn(ct, carry):
        c0 = pl.multiple_of(ct * 128, 128)
        cols = pl.ds(c0, 128)
        scale = base_scale * jnp.exp2(sc_ref[:, cols].astype(F32) * 0.25)
        sct[cols, :] = jnp.broadcast_to(scale, (128, 128)).T
        zpt[cols, :] = jnp.broadcast_to(zp_ref[:, cols].astype(F32), (128, 128)).T
        for rt in range(FEAT // 128):
            rows = slice(rt * 128, rt * 128 + 128)
            vt[cols, rows] = v_ref[rows, cols].T
            ft[cols, rows] = fc_ref[rows, cols].astype(F32).T
            tt[cols, rows] = w_ref[rows, cols].astype(F32).T.astype(BF16)
        return carry

    spread = (
        lax.broadcasted_iota(jnp.int32, (8, FEAT), 1) // BLOCK
        == lax.broadcasted_iota(jnp.int32, (8, FEAT), 0)
    ).astype(F32)
    kept_ref[...] = jnp.dot(
        mask_ref[...].astype(F32).T.astype(BF16), spread.astype(BF16), preferred_element_type=F32
    )
    for copy in inputs:
        copy.wait()
    lax.fori_loop(0, COLS // 128, turn, 0)

    last = NZ - 1

    def way(j):
        return 1 if j % 2 else -1

    def gather_b(j):
        if j == last:
            z_b_last(0, 1).wait_recv()
            z_b_last(1, -1).wait_recv()
        else:
            z_b(j, way(j)).wait_recv()
            if j + 2 < last:
                z_b(j + 2, way(j)).start()
            else:
                z_b_last(0 if way(j) > 0 else 1, way(j)).start()
        for d in (2, 1, 3):
            y_b(j, d).start()

    def last_way(d):
        return 1 if d < 2 else -1

    def gather_a(j, d):
        if j == 0:
            if d:
                y_a(d).wait_recv()
                z_a(1, d, 1).start()
                z_a(2, d, -1).start()
        elif j == last:
            z_a(j, d, last_way(d)).wait_recv()
        else:
            z_a(j, d, way(j)).wait_recv()
            if j + 2 < last:
                z_a(j + 2, d, way(j)).start()
            elif way(j) == last_way(d):
                z_a(last, d, way(j)).start()

    def sibling_step(j):
        for d in (1, 2, 3):
            y_b(j, d).wait_recv()
        sib(j, 1, (db_s, db_r)).start()

    def partial_step(j):
        rows = pl.ds(pl.multiple_of(place(j) * CH, CH), CH)
        acc = None
        for g in range(NY):
            term = lax.dot_general(
                x_buf[g, rows, :], w_all[g], (((1,), (1,)), ((), ())), preferred_element_type=F32
            )
            acc = term if acc is None else acc + term
        r_out[j] = acc.astype(BF16)
        for d in (2, 1, 3):
            rs(j, d).start()

    def sum_step(j):
        mine = pl.ds(pl.multiple_of(x * HALF, 16), HALF)
        total = r_out[j, mine, :].astype(F32)
        for d in (1, 2, 3):
            rs(j, d).wait_recv()
            total = total + r_in[j, d - 1].astype(F32)
        s_all[j, mine, :] = ((2.0 / TOK) * total).astype(BF16)
        for d in (2, 1, 3):
            ag(j, d).start()

    def gradient_step(j):
        for d in (1, 2, 3):
            ag(j, d).wait_recv()
            rs(j, d).wait_send()
            ag(j, d).wait_send()

        @pl.when(j == 0)
        def _():
            g_acc[...] = jnp.zeros_like(g_acc)

        rows = pl.ds(pl.multiple_of(place(j) * CH, CH), CH)
        turned = s_all[j].astype(F32).T.astype(BF16)
        for g in range(NY):
            g_acc[g] += jnp.dot(turned, x_buf[g, rows, :], preferred_element_type=F32)

    def partial_two(u):
        h, j = u // NZ, lax.rem(u, NZ)
        rows = pl.ds(pl.multiple_of(place(j) * CH, CH), CH)
        acc = None
        for g in range(NY):
            term = lax.dot_general(
                x_buf[g, rows, :], w_all[g, half(h), :], (((1,), (1,)), ((), ())),
                preferred_element_type=F32,
            )
            acc = term if acc is None else acc + term
        r2_out[u] = acc.astype(BF16)
        for d in (2, 1, 3):
            rs2(u, d).start()

    def sum_two(u):
        mine = pl.ds(pl.multiple_of(x * HALF, 16), HALF)
        total = r2_out[u, mine, :].astype(F32)
        for d in (1, 2, 3):
            rs2(u, d).wait_recv()
            total = total + r2_in[u, d - 1].astype(F32)
        s2_all[u, mine, :] = ((2.0 / TOK) * total).astype(BF16)
        for d in (2, 1, 3):
            ag2(u, d).start()

    def gradient_two(u):
        h, j = u // NZ, lax.rem(u, NZ)
        for d in (1, 2, 3):
            ag2(u, d).wait_recv()
            rs2(u, d).wait_send()
            ag2(u, d).wait_send()

        @pl.when(j == 0)
        def _():
            g_acc[:, half(h), :] = jnp.zeros((NY, HC, FEAT), F32)

        rows = pl.ds(pl.multiple_of(place(j) * CH, CH), CH)
        turned = s2_all[u].astype(F32).T.astype(BF16)
        for g in range(NY):
            g_acc[g, half(h), :] += jnp.dot(
                turned, x_buf[g, rows, :], preferred_element_type=F32
            )

    def columns(r0):
        rows = pl.ds(r0, UNIT)
        kept = jnp.broadcast_to(kept_ref[pl.ds(r0 // BLOCK, 1), :], (UNIT, FEAT))
        wide = lambda ref: jnp.concatenate([ref[rows, :]] * (FEAT // 128), axis=1)
        return rows, kept, wide(sct), wide(zpt)

    def delta(v, f, t, kept, scale, zero):
        levels = jnp.clip(f + jax.nn.sigmoid(v), 0.0, 15.0)
        return (kept * (scale * (levels - zero) - t)).astype(BF16)

    def first_delta(b, dst):
        def unit(u, carry):
            here = pl.ds(pl.multiple_of(u * UNIT, UNIT), UNIT)
            rows, kept, scale, zero = columns(pl.multiple_of(b * TILE + u * UNIT, UNIT))
            dst[here, :] = delta(
                vt[rows, :], ft[rows, :], tt[rows, :].astype(F32), kept, scale, zero
            )
            return carry

        lax.fori_loop(0, TILE // UNIT, unit, 0)

    def update(b, h, dst):
        def unit(u, carry):
            u0 = pl.multiple_of(h * HC + u * UNIT, UNIT)
            here = pl.ds(u0, UNIT)
            rows, kept, scale, zero = columns(pl.multiple_of(b * TILE + u0, UNIT))
            v, f = vt[rows, :], ft[rows, :]
            relaxed = jax.nn.sigmoid(v)
            in_range = ((f >= 0.0) & (f <= 14.0)).astype(F32)
            centered = 2.0 * relaxed - 1.0
            gradient = g_all[b, here, :].astype(F32)
            descent = gradient * scale * in_range - reg_weight * 8.0 * (
                centered * centered * centered
            )
            v = v - step_rate * kept * descent * relaxed * (1.0 - relaxed)
            vt[rows, :] = v
            if dst is not None:
                dst[here, :] = delta(v, f, tt[rows, :].astype(F32), kept, scale, zero)
            return carry

        lax.fori_loop(0, HC // UNIT, unit, 0)

    def send_gradient(it, h):
        rows = half(h)
        for d in (2, 1, 3):
            b = lax.rem(y + d, NY)
            g_out[b, rows, :] = g_acc[b, rows, :].astype(BF16)
            g_copy(it, h, d).start()
        g_all[y, rows, :] = g_acc[y, rows, :].astype(BF16)

    def refine_half(h):
        update(y, h, w_all.at[y])
        for d in (1, 3, 2):
            g_copy(0, h, d).wait_recv()
            b = lax.rem(y - d + NY, NY)
            update(b, h, w_out.at[b])
            w2_copy(h, NY - d).start()

    def last_update(h):
        update(y, h, None)
        for d in (1, 3, 2):
            g_copy(1, h, d).wait_recv()
            update(lax.rem(y - d + NY, NY), h, None)

    for d in range(NY):
        gather_a(0, d)
    sib(0, 0, (da_s, da_r)).start()
    for d in (2, 1, 3):
        b = lax.rem(y + d, NY)
        first_delta(b, w_out.at[b])
        w_copy(d).start()
    first_delta(y, w_all.at[y])

    def arrive(j):
        sib(j, 0, (da_s, da_r)).wait_recv()
        sib(j, 1, (db_s, db_r)).wait_recv()
        partial_step(j)

    pairs = [(0,), (1, 2), (3, 4), (5, 6), (7,)]
    for k in range(1, 5):
        before, older = pairs[k - 1], pairs[k - 2] if k > 1 else ()
        for j in pairs[k]:
            gather_b(j)
        for d in range(NY):
            for j in pairs[k]:
                gather_a(j, d)
            if d == 0:
                for j in before:
                    sibling_step(j)
                for j in older:
                    sum_step(j)
            if d == 1:
                if k == 1:
                    for e in (1, 2, 3):
                        w_copy(e).wait_recv()
                arrive(before[0])
            if d == 2:
                for j in before[1:]:
                    arrive(j)
            if d == 3:
                for j in pairs[k]:
                    sib(j, 0, (da_s, da_r)).start()
                for j in older:
                    gradient_step(j)
    sibling_step(last)
    for j in pairs[3]:
        sum_step(j)
    arrive(last)
    for j in pairs[3]:
        gradient_step(j)
    sum_step(last)
    gradient_step(last)

    send_gradient(0, 0)
    for d in (1, 2, 3):
        w_copy(d).wait_send()
    refine_half(0)
    send_gradient(0, 1)
    for d in (1, 2, 3):
        w2_copy(0, d).wait_recv()

    def stage_two(s, carry):
        pl.when(s == 2)(lambda: refine_half(1))

        @pl.when(s == NZ)
        def _():
            for d in (1, 2, 3):
                w2_copy(1, d).wait_recv()

        pl.when(s < 2 * NZ)(lambda: partial_two(s))
        pl.when((s >= 2) & (s < 2 * NZ + 2))(lambda: sum_two(s - 2))
        pl.when(s >= 4)(lambda: gradient_two(s - 4))

        @pl.when(s == NZ + 3)
        def _():
            for d in (1, 2, 3):
                g_copy(0, 0, d).wait_send()
            send_gradient(1, 0)

        return carry

    lax.fori_loop(0, 2 * NZ + 4, stage_two, 0)
    for d in (1, 2, 3):
        g_copy(0, 1, d).wait_send()
    send_gradient(1, 1)
    last_update(0)
    last_update(1)

    def turn_back(ct, carry):
        cols = pl.ds(pl.multiple_of(ct * 128, 128), 128)
        for rt in range(FEAT // 128):
            rows = slice(rt * 128, rt * 128 + 128)
            out_ref[rows, cols] = vt[cols, rows].T
        return carry

    lax.fori_loop(0, COLS // 128, turn_back, 0)

    for d in (1, 2, 3):
        y_a(d).wait_send()
        for h in range(2):
            w2_copy(h, d).wait_send()
            g_copy(1, h, d).wait_send()
    for j in range(1, last):
        z_b(j, way(j)).wait_send()
        for d in range(NY):
            z_a(j, d, way(j)).wait_send()
    for d in range(NY):
        z_a(last, d, last_way(d)).wait_send()
    for h in range(2):
        z_b_last(h, 1 - 2 * h).wait_send()

    def drain(j, carry):
        for d in (1, 2, 3):
            y_b(j, d).wait_send()
        sib(j, 0, (da_s, da_r)).wait_send()
        sib(j, 1, (db_s, db_r)).wait_send()
        return carry

    lax.fori_loop(0, NZ, drain, 0)


def per_device(tokens, weight, rounding, floor_codes, scale_codes, zero_codes, block_mask):
    dma = lambda *shape: pltpu.SemaphoreType.DMA(shape)
    pair = lambda *shape: [dma(*shape), dma(*shape)]
    vmem = pl.BlockSpec(memory_space=pltpu.VMEM)
    return pl.pallas_call(
        kernel,
        out_shape=jax.ShapeDtypeStruct((FEAT, COLS), F32),
        in_specs=[vmem] + [pl.BlockSpec(memory_space=pl.ANY)] * 3 + [vmem] * 3,
        out_specs=vmem,
        scratch_shapes=[
            pltpu.VMEM((FEAT, COLS), BF16),
            pltpu.VMEM((FEAT, COLS), F32),
            pltpu.VMEM((FEAT, COLS), jnp.int32),
            pltpu.VMEM((NY, TOK, FEAT), BF16),
            pltpu.VMEM((COLS, FEAT), F32),
            pltpu.VMEM((COLS, FEAT), F32),
            pltpu.VMEM((COLS, FEAT), BF16),
            pltpu.VMEM((COLS, 128), F32),
            pltpu.VMEM((COLS, 128), F32),
            pltpu.VMEM((COLS // BLOCK, FEAT), F32),
            pltpu.VMEM((NY, TILE, FEAT), BF16),
            pltpu.VMEM((NY, TILE, FEAT), BF16),
            pltpu.VMEM((NZ, CH, TILE), BF16),
            pltpu.VMEM((NZ, NX - 1, HALF, TILE), BF16),
            pltpu.VMEM((NZ, CH, TILE), BF16),
            pltpu.VMEM((NY, TILE, FEAT), F32),
            pltpu.VMEM((NY, TILE, FEAT), BF16),
            pltpu.VMEM((NY, TILE, FEAT), BF16),
            pltpu.VMEM((2 * NZ, CH, HC), BF16),
            pltpu.VMEM((2 * NZ, NX - 1, HALF, HC), BF16),
            pltpu.VMEM((2 * NZ, CH, HC), BF16),
            dma(3),
            *pair(3), *pair(NZ, NY), *pair(NZ + 1), *pair(NZ, 3), *pair(NZ), *pair(NZ),
            *pair(3), *pair(2, 3), *pair(NZ, 3), *pair(NZ, 3), *pair(2 * NZ, 3), *pair(2 * NZ, 3),
            *pair(ITERS, 2, 3),
        ],
        compiler_params=pltpu.CompilerParams(
            collective_id=0, has_side_effects=True, vmem_limit_bytes=60 << 20
        ),
        cost_estimate=pl.CostEstimate(
            flops=4 * 2 * TOK * FEAT * COLS, bytes_accessed=8 << 20, transcendentals=4 * FEAT * COLS
        ),
        name="adaround",
    )(
        tokens, weight, rounding, floor_codes,
        scale_codes.reshape(1, COLS), zero_codes.reshape(1, COLS), block_mask,
    )


def solution(mesh):
    fine = Mesh(mesh.devices.reshape(NY, NX, NZ, 2), ("y", "x", "z", "core"))
    loop, dp = ("y", "x"), ("z", "core")
    placed = (
        P(dp, loop),
        P(loop, dp),
        P(loop, dp),
        P(loop, dp),
        P(dp),
        P(dp),
        P(loop, dp),
    )
    return jax.shard_map(
        per_device, mesh=fine, in_specs=placed, out_specs=P(loop, dp), check_vma=False
    )
```

```python
import functools

import jax
import jax.numpy as jnp
from jax import lax
from jax.experimental import pallas as pl
from jax.experimental.pallas import tpu as pltpu
from jax.sharding import Mesh
from jax.sharding import PartitionSpec as P

BLOCK = 64
ITERS = 2
step_rate = 20.0
reg_weight = 0.05
base_scale = 0.02

NY, NX, NZ = 4, 4, 8
SIZES = {"y": NY, "x": NX, "z": NZ, "core": 2}
TOK = 3584
SH = 224
HALF = 112
CH = 448
FEAT = 512
COLS = 896
TILE = 224
HC = 112
UNIT = 16
F32, BF16 = jnp.float32, jnp.bfloat16


def neighbour(axis, offset):
    size = SIZES[axis]
    return {axis: lax.rem(lax.axis_index(axis) + offset + size, size)}


def remote(src, dst, send_sem, recv_sem, axis, offset):
    return pltpu.make_async_remote_copy(
        src_ref=src,
        dst_ref=dst,
        send_sem=send_sem,
        recv_sem=recv_sem,
        device_id=neighbour(axis, offset),
        device_id_type=pl.DeviceIdType.MESH,
    )


def kernel(
    tok_ref, w_hbm, v_hbm, fc_hbm, sc_ref, zp_ref, mask_ref, out_ref,
    w_ref, v_ref, fc_ref,
    x_buf, vt, ft, tt, sct, zpt, kept_ref, w_out, w_all, r_out, r_in, s_all, g_acc, g_out, g_all,
    r2_out, r2_in, s2_all, in_sem,
    ya_s, ya_r, za_s, za_r, zb_s, zb_r, yb_s, yb_r, da_s, da_r, db_s, db_r,
    ws_s, ws_r, w2_s, w2_r, rs_s, rs_r, ag_s, ag_r, rs2_s, rs2_r, ag2_s, ag2_r, gs_s, gs_r,
):
    y, x, z, core = (lax.axis_index(name) for name in ("y", "x", "z", "core"))

    inputs = [
        pltpu.make_async_copy(src, dst, in_sem.at[i])
        for i, (src, dst) in enumerate(((v_hbm, v_ref), (fc_hbm, fc_ref), (w_hbm, w_ref)))
    ]
    for copy in inputs:
        copy.start()

    barrier = pltpu.get_barrier_semaphore()
    partners = [("y", d) for d in (1, 2, 3)] + [("x", d) for d in (1, 2, 3)]
    partners += [("z", 1), ("z", -1), ("core", 1)]
    for axis, offset in partners:
        pl.semaphore_signal(
            barrier, 1, device_id=neighbour(axis, offset), device_id_type=pl.DeviceIdType.MESH
        )
    pl.semaphore_wait(barrier, len(partners))

    def place(j):
        off = ((j + 1) // 2) * (1 - 2 * lax.rem(j, 2))
        return lax.rem(z + off + NZ, NZ)

    def part(zz, cc, b, first=0, rows=HALF):
        return pl.ds(pl.multiple_of((zz * 2 + cc) * SH + b * HALF + first, 16), rows)

    def y_a(d):
        ref = x_buf.at[y, part(z, core, 0)]
        return remote(ref, ref, ya_s.at[d - 1], ya_r.at[d - 1], "y", d)

    def z_a(j, d, direction):
        ref = x_buf.at[lax.rem(y - d + NY, NY), part(place_sent(j, direction), core, 0)]
        return remote(ref, ref, za_s.at[j, d], za_r.at[j, d], "z", direction)

    def z_b(j, direction):
        ref = x_buf.at[y, part(place_sent(j, direction), core, 1)]
        return remote(ref, ref, zb_s.at[j], zb_r.at[j], "z", direction)

    def z_b_last(h, direction):
        ref = x_buf.at[y, part(place_sent(NZ - 1, direction), core, 1, 64 * h, (64, 48)[h])]
        return remote(ref, ref, zb_s.at[NZ - 1 + h], zb_r.at[NZ - 1 + h], "z", direction)

    def place_sent(j, direction):
        return lax.rem(z - direction * ((j + 1) // 2 - 1) + NZ, NZ)

    def y_b(j, d):
        ref = x_buf.at[y, part(place(j), core, 1)]
        return remote(ref, ref, yb_s.at[j, d - 1], yb_r.at[j, d - 1], "y", d)

    def sib(j, b, sems):
        ref = x_buf.at[:, part(place(j), core, b)]
        return remote(ref, ref, sems[0].at[j], sems[1].at[j], "core", 1)

    def rs(j, d):
        q = lax.rem(x + d, NX)
        src = r_out.at[j, pl.ds(pl.multiple_of(q * HALF, 16), HALF)]
        return remote(src, r_in.at[j, d - 1], rs_s.at[j, d - 1], rs_r.at[j, d - 1], "x", d)

    def ag(j, d):
        ref = s_all.at[j, pl.ds(pl.multiple_of(x * HALF, 16), HALF)]
        return remote(ref, ref, ag_s.at[j, d - 1], ag_r.at[j, d - 1], "x", d)

    def half(h, first=0):
        return pl.ds(pl.multiple_of(first + h * HC, 16), HC)

    def w_copy(d):
        b = lax.rem(y + d, NY)
        return remote(w_out.at[b], w_all.at[y], ws_s.at[d - 1], ws_r.at[d - 1], "y", d)

    def w2_copy(h, d):
        b = lax.rem(y + d, NY)
        src, dst = w_out.at[b, half(h)], w_all.at[y, half(h)]
        return remote(src, dst, w2_s.at[h, d - 1], w2_r.at[h, d - 1], "y", d)

    def g_copy(it, h, d):
        b = lax.rem(y + d, NY)
        src, dst = g_out.at[b, half(h)], g_all.at[y, half(h)]
        return remote(src, dst, gs_s.at[it, h, d - 1], gs_r.at[it, h, d - 1], "y", d)

    def rs2(u, d):
        q = lax.rem(x + d, NX)
        src = r2_out.at[u, pl.ds(pl.multiple_of(q * HALF, 16), HALF)]
        return remote(src, r2_in.at[u, d - 1], rs2_s.at[u, d - 1], rs2_r.at[u, d - 1], "x", d)

    def ag2(u, d):
        ref = s2_all.at[u, pl.ds(pl.multiple_of(x * HALF, 16), HALF)]
        return remote(ref, ref, ag2_s.at[u, d - 1], ag2_r.at[u, d - 1], "x", d)

    x_buf[y, pl.ds(pl.multiple_of((z * 2 + core) * SH, SH), SH), :] = tok_ref[...]
    for d in (2, 1, 3):
        y_a(d).start()
    z_b(1, 1).start()
    z_b(2, -1).start()
    z_a(1, 0, 1).start()
    z_a(2, 0, -1).start()
    for d in (2, 1, 3):
        y_b(0, d).start()

    def turn(ct, carry):
        c0 = pl.multiple_of(ct * 128, 128)
        cols = pl.ds(c0, 128)
        scale = base_scale * jnp.exp2(sc_ref[cols].astype(F32) * 0.25)
        sct[cols, :] = jnp.broadcast_to(scale[None, :], (128, 128)).T
        zpt[cols, :] = jnp.broadcast_to(zp_ref[cols].astype(F32)[None, :], (128, 128)).T
        for rt in range(FEAT // 128):
            rows = slice(rt * 128, rt * 128 + 128)
            vt[cols, rows] = v_ref[rows, cols].T
            ft[cols, rows] = fc_ref[rows, cols].astype(F32).T
            tt[cols, rows] = w_ref[rows, cols].astype(F32).T.astype(BF16)
        return carry

    spread = (
        lax.broadcasted_iota(jnp.int32, (8, FEAT), 1) // BLOCK
        == lax.broadcasted_iota(jnp.int32, (8, FEAT), 0)
    ).astype(F32)
    kept_ref[...] = jnp.dot(
        mask_ref[...].astype(F32).T.astype(BF16), spread.astype(BF16), preferred_element_type=F32
    )
    for copy in inputs:
        copy.wait()
    lax.fori_loop(0, COLS // 128, turn, 0)

    last = NZ - 1

    def way(j):
        return 1 if j % 2 else -1

    def gather_b(j):
        if j == last:
            z_b_last(0, 1).wait_recv()
            z_b_last(1, -1).wait_recv()
        else:
            z_b(j, way(j)).wait_recv()
            if j + 2 < last:
                z_b(j + 2, way(j)).start()
            else:
                z_b_last(0 if way(j) > 0 else 1, way(j)).start()
        for d in (2, 1, 3):
            y_b(j, d).start()

    def last_way(d):
        return 1 if d < 2 else -1

    def gather_a(j, d):
        if j == 0:
            if d:
                y_a(d).wait_recv()
                z_a(1, d, 1).start()
                z_a(2, d, -1).start()
        elif j == last:
            z_a(j, d, last_way(d)).wait_recv()
        else:
            z_a(j, d, way(j)).wait_recv()
            if j + 2 < last:
                z_a(j + 2, d, way(j)).start()
            elif way(j) == last_way(d):
                z_a(last, d, way(j)).start()

    def sibling_step(j):
        for d in (1, 2, 3):
            y_b(j, d).wait_recv()
        sib(j, 1, (db_s, db_r)).start()

    def partial_step(j):
        rows = pl.ds(pl.multiple_of(place(j) * CH, CH), CH)
        acc = None
        for g in range(NY):
            term = lax.dot_general(
                x_buf[g, rows, :], w_all[g], (((1,), (1,)), ((), ())), preferred_element_type=F32
            )
            acc = term if acc is None else acc + term
        r_out[j] = acc.astype(BF16)
        for d in (2, 1, 3):
            rs(j, d).start()

    def sum_step(j):
        mine = pl.ds(pl.multiple_of(x * HALF, 16), HALF)
        total = r_out[j, mine, :].astype(F32)
        for d in (1, 2, 3):
            rs(j, d).wait_recv()
            total = total + r_in[j, d - 1].astype(F32)
        s_all[j, mine, :] = ((2.0 / TOK) * total).astype(BF16)
        for d in (2, 1, 3):
            ag(j, d).start()

    def gradient_step(j):
        for d in (1, 2, 3):
            ag(j, d).wait_recv()
            rs(j, d).wait_send()
            ag(j, d).wait_send()

        @pl.when(j == 0)
        def _():
            g_acc[...] = jnp.zeros_like(g_acc)

        rows = pl.ds(pl.multiple_of(place(j) * CH, CH), CH)
        turned = s_all[j].astype(F32).T.astype(BF16)
        for g in range(NY):
            g_acc[g] += jnp.dot(turned, x_buf[g, rows, :], preferred_element_type=F32)

    def partial_two(u):
        h, j = u // NZ, lax.rem(u, NZ)
        rows = pl.ds(pl.multiple_of(place(j) * CH, CH), CH)
        acc = None
        for g in range(NY):
            term = lax.dot_general(
                x_buf[g, rows, :], w_all[g, half(h), :], (((1,), (1,)), ((), ())),
                preferred_element_type=F32,
            )
            acc = term if acc is None else acc + term
        r2_out[u] = acc.astype(BF16)
        for d in (2, 1, 3):
            rs2(u, d).start()

    def sum_two(u):
        mine = pl.ds(pl.multiple_of(x * HALF, 16), HALF)
        total = r2_out[u, mine, :].astype(F32)
        for d in (1, 2, 3):
            rs2(u, d).wait_recv()
            total = total + r2_in[u, d - 1].astype(F32)
        s2_all[u, mine, :] = ((2.0 / TOK) * total).astype(BF16)
        for d in (2, 1, 3):
            ag2(u, d).start()

    def gradient_two(u):
        h, j = u // NZ, lax.rem(u, NZ)
        for d in (1, 2, 3):
            ag2(u, d).wait_recv()
            rs2(u, d).wait_send()
            ag2(u, d).wait_send()

        @pl.when(j == 0)
        def _():
            g_acc[:, half(h), :] = jnp.zeros((NY, HC, FEAT), F32)

        rows = pl.ds(pl.multiple_of(place(j) * CH, CH), CH)
        turned = s2_all[u].astype(F32).T.astype(BF16)
        for g in range(NY):
            g_acc[g, half(h), :] += jnp.dot(
                turned, x_buf[g, rows, :], preferred_element_type=F32
            )

    def columns(r0):
        rows = pl.ds(r0, UNIT)
        kept = jnp.broadcast_to(kept_ref[pl.ds(r0 // BLOCK, 1), :], (UNIT, FEAT))
        wide = lambda ref: jnp.concatenate([ref[rows, :]] * (FEAT // 128), axis=1)
        return rows, kept, wide(sct), wide(zpt)

    def delta(v, f, t, kept, scale, zero):
        levels = jnp.clip(f + jax.nn.sigmoid(v), 0.0, 15.0)
        return (kept * (scale * (levels - zero) - t)).astype(BF16)

    def first_delta(b, dst):
        def unit(u, carry):
            here = pl.ds(pl.multiple_of(u * UNIT, UNIT), UNIT)
            rows, kept, scale, zero = columns(pl.multiple_of(b * TILE + u * UNIT, UNIT))
            dst[here, :] = delta(
                vt[rows, :], ft[rows, :], tt[rows, :].astype(F32), kept, scale, zero
            )
            return carry

        lax.fori_loop(0, TILE // UNIT, unit, 0)

    def update(b, h, dst):
        def unit(u, carry):
            u0 = pl.multiple_of(h * HC + u * UNIT, UNIT)
            here = pl.ds(u0, UNIT)
            rows, kept, scale, zero = columns(pl.multiple_of(b * TILE + u0, UNIT))
            v, f = vt[rows, :], ft[rows, :]
            relaxed = jax.nn.sigmoid(v)
            in_range = ((f >= 0.0) & (f <= 14.0)).astype(F32)
            centered = 2.0 * relaxed - 1.0
            gradient = g_all[b, here, :].astype(F32)
            descent = gradient * scale * in_range - reg_weight * 8.0 * (
                centered * centered * centered
            )
            v = v - step_rate * kept * descent * relaxed * (1.0 - relaxed)
            vt[rows, :] = v
            if dst is not None:
                dst[here, :] = delta(v, f, tt[rows, :].astype(F32), kept, scale, zero)
            return carry

        lax.fori_loop(0, HC // UNIT, unit, 0)

    def send_gradient(it, h):
        rows = half(h)
        for d in (2, 1, 3):
            b = lax.rem(y + d, NY)
            g_out[b, rows, :] = g_acc[b, rows, :].astype(BF16)
            g_copy(it, h, d).start()
        g_all[y, rows, :] = g_acc[y, rows, :].astype(BF16)

    def refine_half(h):
        update(y, h, w_all.at[y])
        for d in (1, 3, 2):
            g_copy(0, h, d).wait_recv()
            b = lax.rem(y - d + NY, NY)
            update(b, h, w_out.at[b])
            w2_copy(h, NY - d).start()

    def last_update(h):
        update(y, h, None)
        for d in (1, 3, 2):
            g_copy(1, h, d).wait_recv()
            update(lax.rem(y - d + NY, NY), h, None)

    for d in range(NY):
        gather_a(0, d)
    sib(0, 0, (da_s, da_r)).start()
    for d in (2, 1, 3):
        b = lax.rem(y + d, NY)
        first_delta(b, w_out.at[b])
        w_copy(d).start()
    first_delta(y, w_all.at[y])

    def arrive(j):
        sib(j, 0, (da_s, da_r)).wait_recv()
        sib(j, 1, (db_s, db_r)).wait_recv()
        partial_step(j)

    pairs = [(0,), (1, 2), (3, 4), (5, 6), (7,)]
    ahead = {1: {0: 2, 2: 3}, 2: {0: 4}, 3: {}, 4: {}}
    for j in pairs[1]:
        gather_b(j)
    for k in range(1, 5):
        before, older = pairs[k - 1], pairs[k - 2] if k > 1 else ()
        for d in range(NY):
            for j in pairs[k]:
                gather_a(j, d)
            if d in ahead[k]:
                for j in pairs[ahead[k][d]]:
                    gather_b(j)
            if d == 0:
                for j in before:
                    sibling_step(j)
                for j in older:
                    sum_step(j)
            if d == 1:
                if k == 1:
                    for e in (1, 2, 3):
                        w_copy(e).wait_recv()
                arrive(before[0])
            if d == 2:
                for j in before[1:]:
                    arrive(j)
            if d == 3:
                for j in pairs[k]:
                    sib(j, 0, (da_s, da_r)).start()
                for j in older:
                    gradient_step(j)
    sibling_step(last)
    for j in pairs[3]:
        sum_step(j)
    arrive(last)
    for j in pairs[3]:
        gradient_step(j)
    sum_step(last)
    gradient_step(last)

    send_gradient(0, 0)
    for d in (1, 2, 3):
        w_copy(d).wait_send()
    refine_half(0)
    send_gradient(0, 1)
    for d in (1, 2, 3):
        w2_copy(0, d).wait_recv()

    def stage_two(s, carry):
        pl.when(s == 2)(lambda: refine_half(1))

        @pl.when(s == NZ)
        def _():
            for d in (1, 2, 3):
                w2_copy(1, d).wait_recv()

        pl.when(s < 2 * NZ)(lambda: partial_two(s))
        pl.when((s >= 4) & (s < 2 * NZ + 4))(lambda: sum_two(s - 4))
        pl.when(s >= 8)(lambda: gradient_two(s - 8))

        @pl.when(s == NZ + 7)
        def _():
            for d in (1, 2, 3):
                g_copy(0, 0, d).wait_send()
            send_gradient(1, 0)

        return carry

    lax.fori_loop(0, 2 * NZ + 8, stage_two, 0)
    for d in (1, 2, 3):
        g_copy(0, 1, d).wait_send()
    send_gradient(1, 1)
    last_update(0)
    last_update(1)

    def turn_back(ct, carry):
        cols = pl.ds(pl.multiple_of(ct * 128, 128), 128)
        for rt in range(FEAT // 128):
            rows = slice(rt * 128, rt * 128 + 128)
            out_ref[rows, cols] = vt[cols, rows].T
        return carry

    lax.fori_loop(0, COLS // 128, turn_back, 0)

    for d in (1, 2, 3):
        y_a(d).wait_send()
        for h in range(2):
            w2_copy(h, d).wait_send()
            g_copy(1, h, d).wait_send()
    for j in range(1, last):
        z_b(j, way(j)).wait_send()
        for d in range(NY):
            z_a(j, d, way(j)).wait_send()
    for d in range(NY):
        z_a(last, d, last_way(d)).wait_send()
    for h in range(2):
        z_b_last(h, 1 - 2 * h).wait_send()

    def drain(j, carry):
        for d in (1, 2, 3):
            y_b(j, d).wait_send()
        sib(j, 0, (da_s, da_r)).wait_send()
        sib(j, 1, (db_s, db_r)).wait_send()
        return carry

    lax.fori_loop(0, NZ, drain, 0)


def per_device(tokens, weight, rounding, floor_codes, scale_codes, zero_codes, block_mask):
    dma = lambda *shape: pltpu.SemaphoreType.DMA(shape)
    pair = lambda *shape: [dma(*shape), dma(*shape)]
    vmem = pl.BlockSpec(memory_space=pltpu.VMEM)
    return pl.pallas_call(
        kernel,
        out_shape=jax.ShapeDtypeStruct((FEAT, COLS), F32),
        in_specs=[vmem] + [pl.BlockSpec(memory_space=pl.ANY)] * 3 + [vmem] * 3,
        out_specs=vmem,
        scratch_shapes=[
            pltpu.VMEM((FEAT, COLS), BF16),
            pltpu.VMEM((FEAT, COLS), F32),
            pltpu.VMEM((FEAT, COLS), jnp.int32),
            pltpu.VMEM((NY, TOK, FEAT), BF16),
            pltpu.VMEM((COLS, FEAT), F32),
            pltpu.VMEM((COLS, FEAT), F32),
            pltpu.VMEM((COLS, FEAT), BF16),
            pltpu.VMEM((COLS, 128), F32),
            pltpu.VMEM((COLS, 128), F32),
            pltpu.VMEM((COLS // BLOCK, FEAT), F32),
            pltpu.VMEM((NY, TILE, FEAT), BF16),
            pltpu.VMEM((NY, TILE, FEAT), BF16),
            pltpu.VMEM((NZ, CH, TILE), BF16),
            pltpu.VMEM((NZ, NX - 1, HALF, TILE), BF16),
            pltpu.VMEM((NZ, CH, TILE), BF16),
            pltpu.VMEM((NY, TILE, FEAT), F32),
            pltpu.VMEM((NY, TILE, FEAT), BF16),
            pltpu.VMEM((NY, TILE, FEAT), BF16),
            pltpu.VMEM((2 * NZ, CH, HC), BF16),
            pltpu.VMEM((2 * NZ, NX - 1, HALF, HC), BF16),
            pltpu.VMEM((2 * NZ, CH, HC), BF16),
            dma(3),
            *pair(3), *pair(NZ, NY), *pair(NZ + 1), *pair(NZ, 3), *pair(NZ), *pair(NZ),
            *pair(3), *pair(2, 3), *pair(NZ, 3), *pair(NZ, 3), *pair(2 * NZ, 3), *pair(2 * NZ, 3),
            *pair(ITERS, 2, 3),
        ],
        compiler_params=pltpu.CompilerParams(
            collective_id=0, has_side_effects=True, vmem_limit_bytes=60 << 20
        ),
        cost_estimate=pl.CostEstimate(
            flops=4 * 2 * TOK * FEAT * COLS, bytes_accessed=8 << 20, transcendentals=4 * FEAT * COLS
        ),
        name="adaround",
    )(
        tokens, weight, rounding, floor_codes,
        scale_codes, zero_codes, block_mask,
    )


def solution(mesh):
    fine = Mesh(mesh.devices.reshape(NY, NX, NZ, 2), ("y", "x", "z", "core"))
    loop, dp = ("y", "x"), ("z", "core")
    placed = (
        P(dp, loop),
        P(loop, dp),
        P(loop, dp),
        P(loop, dp),
        P(dp),
        P(dp),
        P(loop, dp),
    )
    return jax.shard_map(
        per_device, mesh=fine, in_specs=placed, out_specs=P(loop, dp), check_vma=False
    )
```

```python
import functools

import jax
import jax.numpy as jnp
from jax import lax
from jax.experimental import pallas as pl
from jax.experimental.pallas import tpu as pltpu
from jax.sharding import Mesh
from jax.sharding import PartitionSpec as P

BLOCK = 64
ITERS = 2
step_rate = 20.0
reg_weight = 0.05
base_scale = 0.02

NY, NX, NZ = 4, 4, 8
SIZES = {"y": NY, "x": NX, "z": NZ, "core": 2}
TOK = 3584
SH = 224
HALF = 112
CH = 448
FEAT = 512
COLS = 896
TILE = 224
HC = 112
UNIT = 16
F32, BF16 = jnp.float32, jnp.bfloat16


def neighbour(axis, offset):
    size = SIZES[axis]
    return {axis: lax.rem(lax.axis_index(axis) + offset + size, size)}


def remote(src, dst, send_sem, recv_sem, axis, offset):
    return pltpu.make_async_remote_copy(
        src_ref=src,
        dst_ref=dst,
        send_sem=send_sem,
        recv_sem=recv_sem,
        device_id=neighbour(axis, offset),
        device_id_type=pl.DeviceIdType.MESH,
    )


def kernel(
    tok_ref, w_hbm, v_hbm, fc_hbm, sc_ref, zp_ref, mask_ref, out_ref,
    w_ref, v_ref, fc_ref,
    x_buf, vt, ft, tt, sct, zpt, kept_ref, w_out, w_all, r_out, r_in, s_all, g_acc, g_out, g_all,
    r2_out, r2_in, s2_all, in_sem,
    ya_s, ya_r, za_s, za_r, zb_s, zb_r, yb_s, yb_r, da_s, da_r, db_s, db_r,
    ws_s, ws_r, w2_s, w2_r, rs_s, rs_r, ag_s, ag_r, rs2_s, rs2_r, ag2_s, ag2_r, gs_s, gs_r,
):
    y, x, z, core = (lax.axis_index(name) for name in ("y", "x", "z", "core"))

    inputs = [
        pltpu.make_async_copy(src, dst, in_sem.at[i])
        for i, (src, dst) in enumerate(((v_hbm, v_ref), (fc_hbm, fc_ref), (w_hbm, w_ref)))
    ]
    for copy in inputs:
        copy.start()

    barrier = pltpu.get_barrier_semaphore()
    partners = [("y", d) for d in (1, 2, 3)] + [("x", d) for d in (1, 2, 3)]
    partners += [("z", 1), ("z", -1), ("core", 1)]
    for axis, offset in partners:
        pl.semaphore_signal(
            barrier, 1, device_id=neighbour(axis, offset), device_id_type=pl.DeviceIdType.MESH
        )
    pl.semaphore_wait(barrier, len(partners))

    def place(j):
        off = ((j + 1) // 2) * (1 - 2 * lax.rem(j, 2))
        return lax.rem(z + off + NZ, NZ)

    def part(zz, cc, b, first=0, rows=HALF):
        return pl.ds(pl.multiple_of((zz * 2 + cc) * SH + b * HALF + first, 16), rows)

    def y_a(d):
        ref = x_buf.at[y, part(z, core, 0)]
        return remote(ref, ref, ya_s.at[d - 1], ya_r.at[d - 1], "y", d)

    def z_a(j, d, direction):
        ref = x_buf.at[lax.rem(y - d + NY, NY), part(place_sent(j, direction), core, 0)]
        return remote(ref, ref, za_s.at[j, d], za_r.at[j, d], "z", direction)

    def z_b(j, direction):
        ref = x_buf.at[y, part(place_sent(j, direction), core, 1)]
        return remote(ref, ref, zb_s.at[j], zb_r.at[j], "z", direction)

    def z_b_last(h, direction):
        ref = x_buf.at[y, part(place_sent(NZ - 1, direction), core, 1, 64 * h, (64, 48)[h])]
        return remote(ref, ref, zb_s.at[NZ - 1 + h], zb_r.at[NZ - 1 + h], "z", direction)

    def place_sent(j, direction):
        return lax.rem(z - direction * ((j + 1) // 2 - 1) + NZ, NZ)

    def y_b(j, d):
        ref = x_buf.at[y, part(place(j), core, 1)]
        return remote(ref, ref, yb_s.at[j, d - 1], yb_r.at[j, d - 1], "y", d)

    def sib(j, b, sems):
        ref = x_buf.at[:, part(place(j), core, b)]
        return remote(ref, ref, sems[0].at[j], sems[1].at[j], "core", 1)

    def rs(j, d):
        q = lax.rem(x + d, NX)
        src = r_out.at[j, pl.ds(pl.multiple_of(q * HALF, 16), HALF)]
        return remote(src, r_in.at[j, d - 1], rs_s.at[j, d - 1], rs_r.at[j, d - 1], "x", d)

    def ag(j, d):
        ref = s_all.at[j, pl.ds(pl.multiple_of(x * HALF, 16), HALF)]
        return remote(ref, ref, ag_s.at[j, d - 1], ag_r.at[j, d - 1], "x", d)

    def half(h, first=0):
        return pl.ds(pl.multiple_of(first + h * HC, 16), HC)

    def w_copy(d):
        b = lax.rem(y + d, NY)
        return remote(w_out.at[b], w_all.at[y], ws_s.at[d - 1], ws_r.at[d - 1], "y", d)

    def w2_copy(h, d):
        b = lax.rem(y + d, NY)
        src, dst = w_out.at[b, half(h)], w_all.at[y, half(h)]
        return remote(src, dst, w2_s.at[h, d - 1], w2_r.at[h, d - 1], "y", d)

    def g_copy(it, h, d):
        b = lax.rem(y + d, NY)
        src, dst = g_out.at[b, half(h)], g_all.at[y, half(h)]
        return remote(src, dst, gs_s.at[it, h, d - 1], gs_r.at[it, h, d - 1], "y", d)

    def rs2(u, d):
        q = lax.rem(x + d, NX)
        src = r2_out.at[u, pl.ds(pl.multiple_of(q * HALF, 16), HALF)]
        return remote(src, r2_in.at[u, d - 1], rs2_s.at[u, d - 1], rs2_r.at[u, d - 1], "x", d)

    def ag2(u, d):
        ref = s2_all.at[u, pl.ds(pl.multiple_of(x * HALF, 16), HALF)]
        return remote(ref, ref, ag2_s.at[u, d - 1], ag2_r.at[u, d - 1], "x", d)

    x_buf[y, pl.ds(pl.multiple_of((z * 2 + core) * SH, SH), SH), :] = tok_ref[...]
    for d in (2, 1, 3):
        y_a(d).start()
    z_b(1, 1).start()
    z_b(2, -1).start()
    z_a(1, 0, 1).start()
    z_a(2, 0, -1).start()
    for d in (2, 1, 3):
        y_b(0, d).start()

    def turn(ct, carry):
        c0 = pl.multiple_of(ct * 128, 128)
        cols = pl.ds(c0, 128)
        scale = base_scale * jnp.exp2(sc_ref[cols].astype(F32) * 0.25)
        sct[cols, :] = jnp.broadcast_to(scale[None, :], (128, 128)).T
        zpt[cols, :] = jnp.broadcast_to(zp_ref[cols].astype(F32)[None, :], (128, 128)).T
        for rt in range(FEAT // 128):
            rows = slice(rt * 128, rt * 128 + 128)
            vt[cols, rows] = v_ref[rows, cols].T
            ft[cols, rows] = fc_ref[rows, cols].astype(F32).T
            tt[cols, rows] = w_ref[rows, cols].astype(F32).T.astype(BF16)
        return carry

    spread = (
        lax.broadcasted_iota(jnp.int32, (8, FEAT), 1) // BLOCK
        == lax.broadcasted_iota(jnp.int32, (8, FEAT), 0)
    ).astype(F32)
    kept_ref[...] = jnp.dot(
        mask_ref[...].astype(F32).T.astype(BF16), spread.astype(BF16), preferred_element_type=F32
    )
    for copy in inputs:
        copy.wait()
    lax.fori_loop(0, COLS // 128, turn, 0)

    last = NZ - 1

    def way(j):
        return 1 if j % 2 else -1

    def gather_b(j):
        if j == last:
            z_b_last(0, 1).wait_recv()
            z_b_last(1, -1).wait_recv()
        else:
            z_b(j, way(j)).wait_recv()
            if j + 2 < last:
                z_b(j + 2, way(j)).start()
            else:
                z_b_last(0 if way(j) > 0 else 1, way(j)).start()
        for d in (2, 1, 3):
            y_b(j, d).start()

    def last_way(d):
        return 1 if d < 2 else -1

    def gather_a(j, d):
        if j == 0:
            if d:
                y_a(d).wait_recv()
                z_a(1, d, 1).start()
                z_a(2, d, -1).start()
        elif j == last:
            z_a(j, d, last_way(d)).wait_recv()
        else:
            z_a(j, d, way(j)).wait_recv()
            if j + 2 < last:
                z_a(j + 2, d, way(j)).start()
            elif way(j) == last_way(d):
                z_a(last, d, way(j)).start()

    def sibling_step(j):
        for d in (1, 2, 3):
            y_b(j, d).wait_recv()
        sib(j, 1, (db_s, db_r)).start()

    def partial_step(j):
        rows = pl.ds(pl.multiple_of(place(j) * CH, CH), CH)
        acc = None
        for g in range(NY):
            term = lax.dot_general(
                x_buf[g, rows, :], w_all[g], (((1,), (1,)), ((), ())), preferred_element_type=F32
            )
            acc = term if acc is None else acc + term
        r_out[j] = acc.astype(BF16)
        for d in (2, 1, 3):
            rs(j, d).start()

    def sum_step(j):
        mine = pl.ds(pl.multiple_of(x * HALF, 16), HALF)
        total = r_out[j, mine, :].astype(F32)
        for d in (1, 2, 3):
            rs(j, d).wait_recv()
            total = total + r_in[j, d - 1].astype(F32)
        s_all[j, mine, :] = ((2.0 / TOK) * total).astype(BF16)
        for d in (2, 1, 3):
            ag(j, d).start()

    def gradient_step(j):
        for d in (1, 2, 3):
            ag(j, d).wait_recv()
            rs(j, d).wait_send()
            ag(j, d).wait_send()

        @pl.when(j == 0)
        def _():
            g_acc[...] = jnp.zeros_like(g_acc)

        rows = pl.ds(pl.multiple_of(place(j) * CH, CH), CH)
        turned = s_all[j].astype(F32).T.astype(BF16)
        for g in range(NY):
            g_acc[g] += jnp.dot(turned, x_buf[g, rows, :], preferred_element_type=F32)

    def partial_two(u):
        h, j = u // NZ, lax.rem(u, NZ)
        rows = pl.ds(pl.multiple_of(place(j) * CH, CH), CH)
        acc = None
        for g in range(NY):
            term = lax.dot_general(
                x_buf[g, rows, :], w_all[g, half(h), :], (((1,), (1,)), ((), ())),
                preferred_element_type=F32,
            )
            acc = term if acc is None else acc + term
        r2_out[u] = acc.astype(BF16)
        for d in (2, 1, 3):
            rs2(u, d).start()

    def sum_two(u):
        mine = pl.ds(pl.multiple_of(x * HALF, 16), HALF)
        total = r2_out[u, mine, :].astype(F32)
        for d in (1, 2, 3):
            rs2(u, d).wait_recv()
            total = total + r2_in[u, d - 1].astype(F32)
        s2_all[u, mine, :] = ((2.0 / TOK) * total).astype(BF16)
        for d in (2, 1, 3):
            ag2(u, d).start()

    def gradient_two(u):
        h, j = u // NZ, lax.rem(u, NZ)
        for d in (1, 2, 3):
            ag2(u, d).wait_recv()
            rs2(u, d).wait_send()
            ag2(u, d).wait_send()

        @pl.when(j == 0)
        def _():
            g_acc[:, half(h), :] = jnp.zeros((NY, HC, FEAT), F32)

        rows = pl.ds(pl.multiple_of(place(j) * CH, CH), CH)
        turned = s2_all[u].astype(F32).T.astype(BF16)
        for g in range(NY):
            g_acc[g, half(h), :] += jnp.dot(
                turned, x_buf[g, rows, :], preferred_element_type=F32
            )

    def columns(r0):
        rows = pl.ds(r0, UNIT)
        kept = jnp.broadcast_to(kept_ref[pl.ds(r0 // BLOCK, 1), :], (UNIT, FEAT))
        wide = lambda ref: jnp.concatenate([ref[rows, :]] * (FEAT // 128), axis=1)
        return rows, kept, wide(sct), wide(zpt)

    def delta(v, f, t, kept, scale, zero):
        levels = jnp.clip(f + jax.nn.sigmoid(v), 0.0, 15.0)
        return (kept * (scale * (levels - zero) - t)).astype(BF16)

    def first_delta(b, dst):
        def unit(u, carry):
            here = pl.ds(pl.multiple_of(u * UNIT, UNIT), UNIT)
            rows, kept, scale, zero = columns(pl.multiple_of(b * TILE + u * UNIT, UNIT))
            dst[here, :] = delta(
                vt[rows, :], ft[rows, :], tt[rows, :].astype(F32), kept, scale, zero
            )
            return carry

        lax.fori_loop(0, TILE // UNIT, unit, 0)

    def update(b, h, dst):
        def unit(u, carry):
            u0 = pl.multiple_of(h * HC + u * UNIT, UNIT)
            here = pl.ds(u0, UNIT)
            rows, kept, scale, zero = columns(pl.multiple_of(b * TILE + u0, UNIT))
            v, f = vt[rows, :], ft[rows, :]
            relaxed = jax.nn.sigmoid(v)
            in_range = ((f >= 0.0) & (f <= 14.0)).astype(F32)
            centered = 2.0 * relaxed - 1.0
            gradient = g_all[b, here, :].astype(F32)
            descent = gradient * scale * in_range - reg_weight * 8.0 * (
                centered * centered * centered
            )
            v = v - step_rate * kept * descent * relaxed * (1.0 - relaxed)
            vt[rows, :] = v
            if dst is not None:
                dst[here, :] = delta(v, f, tt[rows, :].astype(F32), kept, scale, zero)
            return carry

        lax.fori_loop(0, HC // UNIT, unit, 0)

    def send_gradient(it, h):
        rows = half(h)
        for d in (2, 1, 3):
            b = lax.rem(y + d, NY)
            g_out[b, rows, :] = g_acc[b, rows, :].astype(BF16)
            g_copy(it, h, d).start()
        g_all[y, rows, :] = g_acc[y, rows, :].astype(BF16)

    def refine_half(h):
        update(y, h, w_all.at[y])
        for d in (1, 3, 2):
            g_copy(0, h, d).wait_recv()
            b = lax.rem(y - d + NY, NY)
            update(b, h, w_out.at[b])
            w2_copy(h, NY - d).start()

    def last_update(h):
        update(y, h, None)
        for d in (1, 3, 2):
            g_copy(1, h, d).wait_recv()
            update(lax.rem(y - d + NY, NY), h, None)

    for d in range(NY):
        gather_a(0, d)
    sib(0, 0, (da_s, da_r)).start()
    for d in (2, 1, 3):
        b = lax.rem(y + d, NY)
        first_delta(b, w_out.at[b])
        w_copy(d).start()
    first_delta(y, w_all.at[y])

    def arrive(j):
        sib(j, 0, (da_s, da_r)).wait_recv()
        sib(j, 1, (db_s, db_r)).wait_recv()
        partial_step(j)

    pairs = [(0,), (1, 2), (3, 4), (5, 6), (7,)]
    ahead = {1: {0: 2, 2: 3}, 2: {0: 4}, 3: {}, 4: {}}
    for j in pairs[1]:
        gather_b(j)
    for k in range(1, 5):
        before, older = pairs[k - 1], pairs[k - 2] if k > 1 else ()
        for d in range(NY):
            for j in pairs[k]:
                gather_a(j, d)
            if d in ahead[k]:
                for j in pairs[ahead[k][d]]:
                    gather_b(j)
            if d == 0:
                for j in before:
                    sibling_step(j)
            if d == 1:
                if k == 1:
                    for e in (1, 2, 3):
                        w_copy(e).wait_recv()
                arrive(before[0])
            if d == 2:
                for j in before[1:]:
                    arrive(j)
                for j in older:
                    sum_step(j)
            if d == 3:
                for j in pairs[k]:
                    sib(j, 0, (da_s, da_r)).start()
                for j in pairs[k - 3] if k > 2 else ():
                    gradient_step(j)
    sibling_step(last)
    for j in pairs[3]:
        sum_step(j)
    arrive(last)
    for j in pairs[2] + pairs[3]:
        gradient_step(j)
    sum_step(last)
    gradient_step(last)

    send_gradient(0, 0)
    for d in (1, 2, 3):
        w_copy(d).wait_send()
    refine_half(0)
    send_gradient(0, 1)
    for d in (1, 2, 3):
        w2_copy(0, d).wait_recv()

    def stage_two(s, carry):
        pl.when(s == 4)(lambda: refine_half(1))

        @pl.when(s == NZ)
        def _():
            for d in (1, 2, 3):
                w2_copy(1, d).wait_recv()

        pl.when(s < 2 * NZ)(lambda: partial_two(s))
        pl.when((s >= 4) & (s < 2 * NZ + 4))(lambda: sum_two(s - 4))
        pl.when(s >= 8)(lambda: gradient_two(s - 8))

        @pl.when(s == NZ + 7)
        def _():
            for d in (1, 2, 3):
                g_copy(0, 0, d).wait_send()
            send_gradient(1, 0)

        pl.when(s == 2 * NZ + 3)(lambda: last_update(0))
        return carry

    lax.fori_loop(0, 2 * NZ + 8, stage_two, 0)
    for d in (1, 2, 3):
        g_copy(0, 1, d).wait_send()
    send_gradient(1, 1)
    last_update(1)

    def turn_back(ct, carry):
        cols = pl.ds(pl.multiple_of(ct * 128, 128), 128)
        for rt in range(FEAT // 128):
            rows = slice(rt * 128, rt * 128 + 128)
            out_ref[rows, cols] = vt[cols, rows].T
        return carry

    lax.fori_loop(0, COLS // 128, turn_back, 0)

    for d in (1, 2, 3):
        y_a(d).wait_send()
        for h in range(2):
            w2_copy(h, d).wait_send()
            g_copy(1, h, d).wait_send()
    for j in range(1, last):
        z_b(j, way(j)).wait_send()
        for d in range(NY):
            z_a(j, d, way(j)).wait_send()
    for d in range(NY):
        z_a(last, d, last_way(d)).wait_send()
    for h in range(2):
        z_b_last(h, 1 - 2 * h).wait_send()

    def drain(j, carry):
        for d in (1, 2, 3):
            y_b(j, d).wait_send()
        sib(j, 0, (da_s, da_r)).wait_send()
        sib(j, 1, (db_s, db_r)).wait_send()
        return carry

    lax.fori_loop(0, NZ, drain, 0)


def per_device(tokens, weight, rounding, floor_codes, scale_codes, zero_codes, block_mask):
    dma = lambda *shape: pltpu.SemaphoreType.DMA(shape)
    pair = lambda *shape: [dma(*shape), dma(*shape)]
    vmem = pl.BlockSpec(memory_space=pltpu.VMEM)
    return pl.pallas_call(
        kernel,
        out_shape=jax.ShapeDtypeStruct((FEAT, COLS), F32),
        in_specs=[vmem] + [pl.BlockSpec(memory_space=pl.ANY)] * 3 + [vmem] * 3,
        out_specs=vmem,
        scratch_shapes=[
            pltpu.VMEM((FEAT, COLS), BF16),
            pltpu.VMEM((FEAT, COLS), F32),
            pltpu.VMEM((FEAT, COLS), jnp.int32),
            pltpu.VMEM((NY, TOK, FEAT), BF16),
            pltpu.VMEM((COLS, FEAT), F32),
            pltpu.VMEM((COLS, FEAT), F32),
            pltpu.VMEM((COLS, FEAT), BF16),
            pltpu.VMEM((COLS, 128), F32),
            pltpu.VMEM((COLS, 128), F32),
            pltpu.VMEM((COLS // BLOCK, FEAT), F32),
            pltpu.VMEM((NY, TILE, FEAT), BF16),
            pltpu.VMEM((NY, TILE, FEAT), BF16),
            pltpu.VMEM((NZ, CH, TILE), BF16),
            pltpu.VMEM((NZ, NX - 1, HALF, TILE), BF16),
            pltpu.VMEM((NZ, CH, TILE), BF16),
            pltpu.VMEM((NY, TILE, FEAT), F32),
            pltpu.VMEM((NY, TILE, FEAT), BF16),
            pltpu.VMEM((NY, TILE, FEAT), BF16),
            pltpu.VMEM((2 * NZ, CH, HC), BF16),
            pltpu.VMEM((2 * NZ, NX - 1, HALF, HC), BF16),
            pltpu.VMEM((2 * NZ, CH, HC), BF16),
            dma(3),
            *pair(3), *pair(NZ, NY), *pair(NZ + 1), *pair(NZ, 3), *pair(NZ), *pair(NZ),
            *pair(3), *pair(2, 3), *pair(NZ, 3), *pair(NZ, 3), *pair(2 * NZ, 3), *pair(2 * NZ, 3),
            *pair(ITERS, 2, 3),
        ],
        compiler_params=pltpu.CompilerParams(
            collective_id=0, has_side_effects=True, vmem_limit_bytes=60 << 20
        ),
        cost_estimate=pl.CostEstimate(
            flops=4 * 2 * TOK * FEAT * COLS, bytes_accessed=8 << 20, transcendentals=4 * FEAT * COLS
        ),
        name="adaround",
    )(
        tokens, weight, rounding, floor_codes,
        scale_codes, zero_codes, block_mask,
    )


def solution(mesh):
    fine = Mesh(mesh.devices.reshape(NY, NX, NZ, 2), ("y", "x", "z", "core"))
    loop, dp = ("y", "x"), ("z", "core")
    placed = (
        P(dp, loop),
        P(loop, dp),
        P(loop, dp),
        P(loop, dp),
        P(dp),
        P(dp),
        P(loop, dp),
    )
    return jax.shard_map(
        per_device, mesh=fine, in_specs=placed, out_specs=P(loop, dp), check_vma=False
    )
```
